32 devices in a mesh: blk: 8 (over z, x), pair: 4 (over y, core).
Axes of the slice: x: 2, y: 2, z: 4, core: 2. Of those that a mesh axis runs over, the one named last changes fastest.
Arguments:
- amplitudes: bfloat16 [4, 96, 12, 1024], P('pair', 'blk'), may hold values from -6 to 6
- tile_mask: int32 [4, 96, 12], P('pair', 'blk'), may hold values 0 or 1
- integrals: bfloat16 [64, 1024, 1024], P('blk', 'pair'), may hold values from -0.078125 to 0.078125
- block_tiles: int32 [64, 2], P('blk'), may hold values from 0 to 11
- block_keep: int32 [64], P('blk'), may hold values 0 or 1
- slot_tile: int32 [96], replicated, may hold values from 0 to 95, each once
Outputs:
- ladder: bfloat16 [96, 4, 96, 128], P('blk', 'pair')
The draws below stay inside these ranges and needn't reach their ends.
Inputs may be any that keep to these rules, and one draw needn't show every extreme that they name: `slot_tile`: each result tile appears in exactly one slot.
All inputs are finite; a program needn't handle non-finite values. No bound on the sum of `tile_mask` or of `block_keep` on one device may be relied on, other than what follows from the above.
Results may differ from the reference program's by a relative error of at most 0.013.
Values may be sent and summed in bfloat16 or wider, within the bound.
No kernel may reach another device: no remote copies, remote signals or barrier semaphores. Data moves between devices by JAX's collectives and lax.ppermute only.
A program may use at most 128 MiB of HBM per device.

```python
import jax
import jax.numpy as jnp
from jax import lax

TV = 128
NT = 12
DW = 8
BW = 8
KMAX = 8
SLABS = 4
SLAB_ROWS = 96
BLOCKS = 64
NOUT = 96
N_BLK = 8


def plant(values, rng, least, top_value):
    place = [jax.random.randint(jax.random.fold_in(rng, axis), (), 0, length) for axis, length in enumerate(values.shape)]
    longest = values.shape.index(max(values.shape))
    next_to = place[:longest] + [(place[longest] + 1) % values.shape[longest]] + place[longest + 1:]
    return values.at[tuple(place)].set(least).at[tuple(next_to)].set(top_value)


def block_scale(key, shape, pieces, low, top_value):
    loudness = 1.0
    for dim, blocks in pieces:
        draws = jax.random.uniform(jax.random.fold_in(jax.random.fold_in(key, 6), dim), (blocks,), jnp.float32, low / len(pieces), top_value / len(pieces))
        loudness = loudness * jnp.repeat(jnp.exp(draws), shape[dim] // blocks).reshape((-1,) + (1,) * (len(shape) - 1 - dim))
    return loudness


def scatter_about(stream_key, extent, deviation, reach, pieces=(), held_as=jnp.bfloat16):
    array = jax.random.normal(stream_key, extent, jnp.float32) * deviation
    if len(pieces) > 0:
        array = block_scale(stream_key, extent, pieces, -0.22, 0.18) * array
    return jnp.clip(array, min=-reach, max=reach).astype(held_as)


def setup_inputs(seed: int = 0) -> dict:
    splits = jax.random.split(jax.random.key(seed), 7)
    return {
        "amplitudes": scatter_about(splits[0], (SLABS, SLAB_ROWS, NT, DW * TV), 1.0, 6.0, ((0, 4), (1, 8))),
        "tile_mask": plant((jax.random.randint(splits[1], (SLABS, SLAB_ROWS, NT), 0, 4) < 3).astype(jnp.int32), jax.random.fold_in(splits[1], 1), 0, 1),
        "integrals": scatter_about(splits[2], (BLOCKS, DW * TV, BW * TV), (DW * TV * KMAX * N_BLK // NT) ** -0.5, 0.078125, ((0, 8), (1, 4))),
        "block_tiles": plant(jax.random.randint(splits[3], (BLOCKS, 2), 0, NT), jax.random.fold_in(splits[3], 1), 0, NT - 1).astype(jnp.int32),
        "block_keep": plant((jax.random.randint(splits[4], (BLOCKS,), 0, 4) < 3).astype(jnp.int32), jax.random.fold_in(splits[4], 1), 0, 1),
        "slot_tile": jax.random.permutation(splits[5], NOUT).astype(jnp.int32),
    }


def reference(amplitudes, tile_mask, integrals, block_tiles, block_keep, slot_tile):
    masked = amplitudes * tile_mask.astype(jnp.bfloat16)[..., None]
    flattened = masked.reshape(SLABS * SLAB_ROWS, NT, DW * TV)

    def add_block(total, element):
        integral, pair_tiles, keep_flag = element
        row_block = lax.dynamic_index_in_dim(flattened, pair_tiles[0], 1, False)
        product = jnp.dot(row_block, integral, preferred_element_type=jnp.float32) * keep_flag.astype(jnp.float32)
        current = lax.dynamic_index_in_dim(total, pair_tiles[1], 1, False)
        return lax.dynamic_update_index_in_dim(total, current + product, pair_tiles[1], 1), None

    def add_holder(grand, element):
        begin = jnp.zeros((SLABS * SLAB_ROWS, NT, BW * TV), jnp.float32)
        holder_sum, _ = lax.scan(add_block, begin, element)
        rounded = lax.optimization_barrier(holder_sum.astype(jnp.bfloat16)).astype(jnp.float32)
        return grand + rounded, None

    grouped = (integrals.reshape(N_BLK, KMAX, DW * TV, BW * TV),
               block_tiles.reshape(N_BLK, KMAX, 2),
               block_keep.reshape(N_BLK, KMAX))
    grand = jnp.zeros((SLABS * SLAB_ROWS, NT, BW * TV), jnp.float32)
    grand, _ = lax.scan(add_holder, grand, grouped)
    tile_rows = grand.reshape(SLABS * SLAB_ROWS, NT * BW, TV)
    picked = jnp.take(tile_rows, slot_tile, axis=1)
    result = jnp.transpose(picked, (1, 0, 2)).reshape(NT * BW, SLABS, SLAB_ROWS, TV)
    return result.astype(jnp.bfloat16)
```

```python
import functools

import jax
import jax.numpy as jnp
from jax import lax
from jax.experimental import pallas as pl
from jax.experimental.pallas import tpu as pltpu
from jax.sharding import PartitionSpec as P

LANES = 128


def blk_swap(value, dz, dx, nz, nx):
    pairs = [(z * nx + x, (z ^ dz) * nx + (x ^ dx)) for z in range(nz) for x in range(nx)]
    return lax.ppermute(value, "blk", pairs)


def pair_swap(value, dy, dc, ny, nc):
    pairs = [(y * nc + c, (y ^ dy) * nc + (c ^ dc)) for y in range(ny) for c in range(nc)]
    return lax.ppermute(value, "pair", pairs)


def pick(position, options):
    value = options[0]
    for index in range(1, len(options)):
        value = jnp.where(position == index, options[index], value)
    return value


def product_kernel(nx, nc, rows, ctile, keep, pos, *refs):
    units, blocks, outs = refs[:nx], refs[nx : nx + nc], refs[nx + nc :]
    ny = len(outs)
    x, c = pos[0], pos[1]
    depth = blocks[0].shape[1]
    parts = [unit[0] for unit in units]
    lhs = jnp.concatenate([pick(x ^ at, parts) for at in range(nx)], axis=0)
    total = None
    for d in range(nc):
        which = c ^ d
        columns = pick(which, [lhs[:, i * depth : (i + 1) * depth] for i in range(nc)])
        term = jnp.dot(columns, blocks[d][0], preferred_element_type=jnp.float32)
        total = term if total is None else total + term
    total = total * keep[pl.program_id(0)].astype(jnp.float32)
    for s in range(ny):
        pieces = [total[(at * ny + s) * rows : (at * ny + s + 1) * rows] for at in range(nx)]
        outs[s][0] = jnp.concatenate(pieces, axis=0).astype(outs[s].dtype)


def products(units, blocks, ctile, keep, pos, ny, rows):
    nx, nc = len(units), len(blocks)
    slots, depth, width = blocks[0].shape
    tile_count, unit_rows, unit_columns = units[0].shape
    out = jax.ShapeDtypeStruct((slots, nx * rows, width), jnp.bfloat16)
    return pl.pallas_call(
        functools.partial(product_kernel, nx, nc, rows),
        grid_spec=pltpu.PrefetchScalarGridSpec(
            num_scalar_prefetch=3,
            grid=(slots,),
            in_specs=[pl.BlockSpec((1, unit_rows, unit_columns), lambda k, ct, kp, ps: (ct[k], 0, 0))] * nx
            + [pl.BlockSpec((1, depth, width), lambda k, ct, kp, ps: (k, 0, 0))] * nc,
            out_specs=[pl.BlockSpec((1, nx * rows, width), lambda k, ct, kp, ps: (k, 0, 0))] * ny,
        ),
        out_shape=[out] * ny,
        cost_estimate=pl.CostEstimate(
            flops=2 * slots * nx * unit_rows * unit_columns * width,
            bytes_accessed=2 * slots * nc * depth * width,
            transcendentals=0,
        ),
        compiler_params=pltpu.CompilerParams(vmem_limit_bytes=32 * 2**20),
        name="products",
    )(ctile, keep, pos, *units, *blocks)


def route_kernel(ny, nx, nz, atile, slot_tile, pos, *refs):
    parts, outs, total = refs[:ny], refs[ny : ny + nx], refs[ny + nx]
    x, z = pos[0], pos[2]
    slots = parts[0].shape[0]
    per_tile = total.shape[2] // LANES
    owned = outs[0].shape[0] // nz
    total[...] = jnp.zeros_like(total)

    def add(k, _):
        value = parts[0][k].astype(jnp.float32)
        for part in parts[1:]:
            value += part[k].astype(jnp.float32)
        total[atile[k]] += value
        return 0

    lax.fori_loop(0, slots, add, 0)
    for d in range(nx):
        for dz in range(nz):
            owner = (z ^ dz) * nx + (x ^ d)
            for i in range(owned):
                tile = slot_tile[owner * owned + i]
                a = lax.div(tile, per_tile)
                column = pl.multiple_of(lax.rem(tile, per_tile) * LANES, LANES)
                outs[d][dz * owned + i] = total[a, :, pl.ds(column, LANES)].astype(outs[d].dtype)


def route(parts, atile, slot_tile, pos, tile_count, nx, nz):
    slots, rows, width = parts[0].shape
    result_tiles = slot_tile.shape[0]
    out = jax.ShapeDtypeStruct((result_tiles // nx, rows, LANES), jnp.bfloat16)
    smem = pl.BlockSpec(memory_space=pltpu.SMEM)
    vmem = pl.BlockSpec(memory_space=pltpu.VMEM)
    return pl.pallas_call(
        functools.partial(route_kernel, len(parts), nx, nz),
        in_specs=[smem] * 3 + [vmem] * len(parts),
        out_specs=[vmem] * nx,
        out_shape=[out] * nx,
        scratch_shapes=[pltpu.VMEM((tile_count, rows, width), jnp.float32)],
        cost_estimate=pl.CostEstimate(
            flops=2 * slots * rows * width, bytes_accessed=4 * slots * rows * width, transcendentals=0
        ),
        compiler_params=pltpu.CompilerParams(vmem_limit_bytes=32 * 2**20),
        name="route",
    )(atile, slot_tile, pos, *parts)


def add_kernel(n, *refs):
    parts, outs = refs[:n], refs[n:]
    value = parts[0][...].astype(jnp.float32)
    for part in parts[1:]:
        value += part[...].astype(jnp.float32)
    count = outs[0].shape[0]
    for i, out in enumerate(outs):
        out[...] = value[i * count : (i + 1) * count].astype(out.dtype)


def add_split(parts, nz):
    tiles, rows, lanes = parts[0].shape
    out = jax.ShapeDtypeStruct((tiles // nz, rows, lanes), jnp.bfloat16)
    vmem = pl.BlockSpec(memory_space=pltpu.VMEM)
    return pl.pallas_call(
        functools.partial(add_kernel, len(parts)),
        in_specs=[vmem] * len(parts),
        out_specs=[vmem] * nz,
        out_shape=[out] * nz,
        cost_estimate=pl.CostEstimate(
            flops=tiles * rows * lanes, bytes_accessed=4 * tiles * rows * lanes, transcendentals=0
        ),
        compiler_params=pltpu.CompilerParams(vmem_limit_bytes=32 * 2**20),
        name="add_split",
    )(*parts)


def final_kernel(nz, pos, *refs):
    out = refs[-1]
    z = pos[2]
    for ahead in range(nz):
        value = None
        for e in range(nz):
            term = refs[e * nz + (e ^ ahead)][...].astype(jnp.float32)
            value = term if value is None else value + term
        out[:, z ^ ahead] = value.astype(out.dtype)


def final_sum(received, pos, nz):
    owned, rows, lanes = received[0][0].shape
    smem = pl.BlockSpec(memory_space=pltpu.SMEM)
    vmem = pl.BlockSpec(memory_space=pltpu.VMEM)
    return pl.pallas_call(
        functools.partial(final_kernel, nz),
        in_specs=[smem] + [vmem] * (nz * nz),
        out_specs=vmem,
        out_shape=jax.ShapeDtypeStruct((owned, nz, rows, lanes), jnp.bfloat16),
        compiler_params=pltpu.CompilerParams(vmem_limit_bytes=32 * 2**20),
        name="final_sum",
    )(pos, *[part for line in received for part in line])


def per_device(nz, nx, ny, nc, amplitudes, tile_mask, integrals, block_tiles, block_keep, slot_tile):
    blk, pair = lax.axis_index("blk"), lax.axis_index("pair")
    z, x, y, c = blk // nx, blk % nx, pair // nc, pair % nc
    pos = jnp.stack([x, c, z]).astype(jnp.int32)
    ctile, atile = block_tiles[:, 0], block_tiles[:, 1]
    _, rows, tile_count, contracted = amplitudes.shape
    columns = contracted // ny

    blocks = [integrals] + [pair_swap(integrals, 0, d, ny, nc) for d in range(1, nc)]

    masked = amplitudes[0] * tile_mask[0].astype(jnp.bfloat16)[:, :, None]
    masked = masked.transpose(1, 0, 2)
    pieces = []
    for d in range(ny):
        piece = lax.dynamic_slice_in_dim(masked, (y ^ d) * columns, columns, axis=2)
        pieces.append(pair_swap(piece, d, 0, ny, nc) if d else piece)
    unit = jnp.concatenate(pieces, axis=1)

    received = [[None] * nz for _ in range(nz)]
    for dz in range(nz):
        here = blk_swap(unit, dz, 0, nz, nx) if dz else unit
        units = [here] + [blk_swap(here, 0, d, nz, nx) for d in range(1, nx)]
        partial = products(units, blocks, ctile, block_keep, pos, ny, rows)
        parts = [partial[0]] + [pair_swap(partial[d], d, 0, ny, nc) for d in range(1, ny)]
        by_owner = route(parts, atile, slot_tile, pos, tile_count, nx, nz)
        mine = [by_owner[0]] + [blk_swap(by_owner[d], 0, d, nz, nx) for d in range(1, nx)]
        to_column = add_split(mine, nz)
        for e in range(nz):
            received[e][dz] = blk_swap(to_column[e], e, 0, nz, nx) if e else to_column[0]
    out = final_sum(received, pos, nz)
    return out.reshape(out.shape[0], 1, out.shape[1] * out.shape[2], LANES)


def solution(mesh):
    holders, pairs = mesh.shape["blk"], mesh.shape["pair"]
    nx = 1
    while (2 * nx) ** 2 <= holders:
        nx *= 2
    nc = 2 if pairs % 2 == 0 else 1
    placed = (
        P("pair", "blk", None, None),
        P("pair", "blk", None),
        P("blk", "pair", None),
        P("blk", None),
        P("blk"),
        P(),
    )
    return jax.shard_map(
        functools.partial(per_device, holders // nx, nx, pairs // nc, nc),
        mesh=mesh,
        in_specs=placed,
        out_specs=P("blk", "pair", None, None),
        check_vma=False,
    )
```

```python
import functools

import jax
import jax.numpy as jnp
from jax import lax
from jax.experimental import pallas as pl
from jax.experimental.pallas import tpu as pltpu
from jax.sharding import PartitionSpec as P

LANES = 128
SMEM = pl.BlockSpec(memory_space=pltpu.SMEM)
VMEM = pl.BlockSpec(memory_space=pltpu.VMEM)
ANY = pl.BlockSpec(memory_space=pl.ANY)
GRANT = 32 * 2**20
WEIGHT = 20_000_000_000


def blk_swap(value, dz, dx, nz, nx):
    pairs = [(z * nx + x, (z ^ dz) * nx + (x ^ dx)) for z in range(nz) for x in range(nx)]
    return lax.ppermute(value, "blk", pairs)


def slab_swap(value, dx, dy, nz, nx, ny, nc):
    pairs = [
        (((z * nx + x) * ny + y) * nc + c, ((z * nx + (x ^ dx)) * ny + (y ^ dy)) * nc + c)
        for z in range(nz)
        for x in range(nx)
        for y in range(ny)
        for c in range(nc)
    ]
    return lax.ppermute(value, ("blk", "pair"), pairs)


def pair_swap(value, dy, dc, ny, nc):
    pairs = [(y * nc + c, (y ^ dy) * nc + (c ^ dc)) for y in range(ny) for c in range(nc)]
    return lax.ppermute(value, "pair", pairs)


def pick(position, options):
    value = options[0]
    for index in range(1, len(options)):
        value = jnp.where(position == index, options[index], value)
    return value


def bf16(*shape):
    return jax.ShapeDtypeStruct(shape, jnp.bfloat16)


class Step:
    def __init__(self, body, scalars, arrays, outs, scratch=()):
        self.body, self.scalars, self.arrays = body, list(scalars), list(arrays)
        self.outs, self.scratch = list(outs), list(scratch)


def launch(name, steps, after):
    scalars, arrays = [], []
    for step in steps:
        for value in step.scalars:
            if not any(value is other for other in scalars):
                scalars.append(value)
        for value in step.arrays:
            if not any(value is other for other in arrays):
                arrays.append(value)
    operands = scalars + arrays
    find = lambda value: next(i for i, other in enumerate(operands) if other is value)
    outs = [out for step in steps for out in step.outs]
    scratch = [s for step in steps for s in step.scratch]

    def kernel(*refs):
        out_refs = refs[len(operands) + len(after) :]
        scratch_refs = out_refs[len(outs) :]
        o = s = 0
        for step in steps:
            step.body(
                [refs[find(value)] for value in step.scalars],
                [refs[find(value)] for value in step.arrays],
                out_refs[o : o + len(step.outs)],
                scratch_refs[s : s + len(step.scratch)],
            )
            o, s = o + len(step.outs), s + len(step.scratch)

    results = pl.pallas_call(
        kernel,
        in_specs=[SMEM] * len(scalars) + [VMEM] * len(arrays) + [ANY] * len(after),
        out_specs=[VMEM] * len(outs),
        out_shape=outs,
        scratch_shapes=scratch,
        cost_estimate=pl.CostEstimate(flops=WEIGHT, bytes_accessed=0, transcendentals=0),
        compiler_params=pltpu.CompilerParams(vmem_limit_bytes=GRANT),
        name=name,
    )(*operands, *after)
    split, o = [], 0
    for step in steps:
        split.append(results[o : o + len(step.outs)])
        o += len(step.outs)
    return split


class Meta:
    def __init__(self, slots):
        self.ctile, self.atile, self.keep = 0, slots, 2 * slots
        self.x, self.c, self.z = (3 * slots + i for i in range(3))


def join(parts):
    tiles, rows, columns = parts[0].shape

    def body(_, refs, outs, __):
        outs[0][...] = jnp.concatenate([ref[...] for ref in refs], axis=1)

    return Step(body, [], parts, [bf16(tiles, rows * len(parts), columns)])


def hold(values, after):
    def kernel(*refs):
        sources, outs, sems = refs[: len(values)], refs[len(values) + len(after) : -1], refs[-1]
        copies = [pltpu.make_async_copy(s, o, sems.at[i]) for i, (s, o) in enumerate(zip(sources, outs, strict=True))]
        for copy in copies:
            copy.start()
        for copy in copies:
            copy.wait()

    return pl.pallas_call(
        kernel,
        in_specs=[ANY] * (len(values) + len(after)),
        out_specs=[VMEM] * len(values),
        out_shape=[bf16(*value.shape) for value in values],
        scratch_shapes=[pltpu.SemaphoreType.DMA((len(values),))],
        cost_estimate=pl.CostEstimate(flops=WEIGHT, bytes_accessed=0, transcendentals=0),
        compiler_params=pltpu.CompilerParams(vmem_limit_bytes=GRANT),
        name="hold",
    )(*values, *after)


def pack(ctile, here):
    slots = ctile.shape[0]

    def body(scalars, refs, outs, _):
        for k in range(slots):
            outs[0][k] = refs[0][scalars[0][k]]

    return Step(body, [ctile], [here], [bf16(slots, *here.shape[1:])])


def through(value):
    def body(_, refs, outs, __):
        outs[0][...] = refs[0][...]

    return Step(body, [], [value], [bf16(*value.shape)])


def products(meta, at, here, others, blocks, ny, rows):
    nx, nc = 1 + len(others), len(blocks)
    slots, depth, width = blocks[0].shape
    whole = isinstance(others[0], list)
    flat = [o for other in others for o in other] if whole else list(others)
    each = len(others[0]) if whole else 1

    def body(scalars, refs, outs, _):
        meta_ref = scalars[0]
        here_ref, other_refs, block_refs = refs[0], refs[1 : 1 + len(flat)], refs[1 + len(flat) :]
        x, c = meta_ref[at.x], meta_ref[at.c]
        for k in range(slots):
            tile = meta_ref[at.ctile + k]
            parts = [here_ref[tile]]
            for d in range(nx - 1):
                pieces = [ref[tile if whole else k] for ref in other_refs[d * each : (d + 1) * each]]
                parts.append(jnp.concatenate(pieces, axis=0) if whole else pieces[0])
            lhs = jnp.concatenate([pick(x ^ i, parts) for i in range(nx)], axis=0)
            total = None
            for d in range(nc):
                columns = pick(c ^ d, [lhs[:, i * depth : (i + 1) * depth] for i in range(nc)])
                term = jnp.dot(columns, block_refs[d][k], preferred_element_type=jnp.float32)
                total = term if total is None else total + term
            total = total * meta_ref[at.keep + k].astype(jnp.float32)
            for s in range(ny):
                pieces = [total[(i * ny + s) * rows : (i * ny + s + 1) * rows] for i in range(nx)]
                outs[s][k] = jnp.concatenate(pieces, axis=0).astype(outs[s].dtype)

    return Step(body, [meta], [here, *flat, *blocks], [bf16(slots, nx * rows, width)] * ny)


def route(meta, at, slot_tile, parts, tile_count, nx, nz):
    slots, rows, width = parts[0].shape
    owned = slot_tile.shape[0] // (nx * nz)
    per_tile = width // LANES

    def body(scalars, refs, outs, scratch):
        meta_ref, slot_ref = scalars
        total = scratch[0]
        x, z = meta_ref[at.x], meta_ref[at.z]
        total[...] = jnp.zeros_like(total)

        def add(k, _):
            value = refs[0][k].astype(jnp.float32)
            for ref in refs[1:]:
                value += ref[k].astype(jnp.float32)
            total[meta_ref[at.atile + k]] += value
            return 0

        lax.fori_loop(0, slots, add, 0)
        for d in range(nx):
            for dz in range(nz):
                owner = (z ^ dz) * nx + (x ^ d)
                for i in range(owned):
                    tile = slot_ref[owner * owned + i]
                    a = lax.div(tile, per_tile)
                    column = pl.multiple_of(lax.rem(tile, per_tile) * LANES, LANES)
                    outs[d][dz * owned + i] = total[a, :, pl.ds(column, LANES)].astype(outs[d].dtype)

    scratch = [pltpu.VMEM((tile_count, rows, width), jnp.float32)]
    return Step(body, [meta, slot_tile], parts, [bf16(nz * owned, rows, LANES)] * nx, scratch)


def add_split(chunks, nz):
    tiles, rows, lanes = chunks[0][0].shape
    count, each = tiles // nz, len(chunks[0])

    def body(_, refs, outs, __):
        for i in range(len(chunks)):
            for e, out in enumerate(outs):
                span = slice(e * count, (e + 1) * count)
                value = refs[i * each][span].astype(jnp.float32)
                for part in refs[i * each + 1 : (i + 1) * each]:
                    value += part[span].astype(jnp.float32)
                out[:, i] = value.astype(out.dtype)

    flat = [part for chunk in chunks for part in chunk]
    return Step(body, [], flat, [bf16(count, len(chunks), rows, lanes)] * nz)


def final_sum(meta, at, received, groups, nz):
    owned, _, rows, lanes = received[0][0].shape
    where = {d: (g, i) for g, group in enumerate(groups) for i, d in enumerate(group)}

    def body(scalars, refs, outs, _):
        z = scalars[0][at.z]
        for ahead in range(nz):
            value = None
            for e in range(nz):
                g, i = where[e ^ ahead]
                term = refs[g * nz + e][:, i].astype(jnp.float32)
                value = term if value is None else value + term
            outs[0][:, z ^ ahead] = value.astype(outs[0].dtype)

    flat = [part for line in received for part in line]
    return Step(body, [meta], flat, [bf16(owned, nz, rows, lanes)])


def per_device(nz, nx, ny, nc, amplitudes, tile_mask, integrals, block_tiles, block_keep, slot_tile):
    blk, pair = lax.axis_index("blk"), lax.axis_index("pair")
    z, x, y, c = blk // nx, blk % nx, pair // nc, pair % nc
    _, rows, tile_count, contracted = amplitudes.shape
    slots = block_keep.shape[0]
    columns = contracted // ny
    at = Meta(slots)

    blocks = [integrals] + [pair_swap(integrals, 0, d, ny, nc) for d in range(1, nc)]
    ctile = block_tiles[:, 0]
    place = jnp.stack([x, c, z]).astype(jnp.int32)
    meta = jnp.concatenate([ctile, block_tiles[:, 1], block_keep, place])
    their_ctile = [blk_swap(ctile, 0, d, nz, nx) for d in range(1, nx)]

    masked = amplitudes[0] * tile_mask[0].astype(jnp.bfloat16)[:, :, None]
    masked = masked.transpose(1, 0, 2)
    pieces = [lax.dynamic_slice_in_dim(masked, (y ^ d) * columns, columns, axis=2) for d in range(ny)]

    here, others, partial, by_owner, received = {}, {}, {}, {}, []
    last = []

    def run(name, *steps):
        nonlocal last
        results = launch(name, [step for step, _ in steps], last)
        last = results[0][:1]
        for (_, use), result in zip(steps, results, strict=True):
            use(result)

    def do_join(from_y):
        def use(out):
            here[0] = out[0]
            here[1] = blk_swap(out[0], 1, 0, nz, nx)

        return join(from_y), use

    def do_relay(d, s):
        def use(out):
            others[0][d - 1].append(blk_swap(out[0], 0, d, nz, nx))

        return through(from_y[s]), use

    def do_spread():
        def use(out):
            for d in range(2, nz):
                if d & -d == d:
                    here[d] = blk_swap(out[0], d, 0, nz, nx)

        return through(here[0]), use

    def do_pack(d, i):
        def use(out):
            others.setdefault(d, {})[i] = blk_swap(out[0], 0, i, nz, nx)

        return pack(their_ctile[i - 1], here[d]), use

    def do_forward(d):
        def use(out):
            for step in range(1, d & -d):
                if step & -step == step:
                    here[d | step] = blk_swap(out[0], step, 0, nz, nx)

        return through(here[d]), use

    def do_products(d):
        def use(out):
            partial[d] = [out[0]] + [pair_swap(out[i], i, 0, ny, nc) for i in range(1, ny)]

        rest = others[d] if isinstance(others[d], list) else [others[d][i] for i in range(1, nx)]
        return products(meta, at, here[d], rest, blocks, ny, rows), use

    def do_route(d):
        def use(out):
            by_owner[d] = [out[0]] + [blk_swap(out[i], 0, i, nz, nx) for i in range(1, nx)]

        return route(meta, at, slot_tile, partial[d], tile_count, nx, nz), use

    def do_add(group):
        def use(out):
            received.append([out[0]] + [blk_swap(out[e], e, 0, nz, nx) for e in range(1, nz)])

        return add_split([by_owner[d] for d in group], nz), use

    from_y = [pieces[0]] + [pair_swap(pieces[d], d, 0, ny, nc) for d in range(1, ny)]
    others[0] = [[blk_swap(from_y[0], 0, dx, nz, nx)] for dx in range(1, nx)]
    blocks = [blocks[0], *hold(blocks[1:], pieces[:1])] if nc > 1 else blocks
    last = blocks[1:2]
    run("join", do_join(from_y), *[do_relay(d, s) for d in range(1, nx) for s in range(1, ny)])
    last = [last[0], *[other[0] for other in others[0]]]
    run("spread", do_spread())
    slots_of, groups = plan(nz)
    for slot in slots_of:
        steps = []
        for what, d in slot:
            if what == "arrive":
                steps += [do_pack(d, i) for i in range(1, nx)]
            elif what == "forward":
                steps.append(do_forward(d))
            else:
                steps.append({"multiply": do_products, "route": do_route, "add": do_add}[what](d))
        run("_".join(what for what, _ in slot), *steps)
    out = launch("final_sum", [final_sum(meta, at, received, groups, nz)], last)[0][0]
    return out.reshape(out.shape[0], 1, out.shape[1] * out.shape[2], LANES)


def plan(nz):
    m, r, a, f, s = "multiply", "route", "arrive", "forward", "add"
    if nz == 4:
        return [
            [(m, 0)],
            [(a, 1)],
            [(f, 2)],
            [(r, 0)],
            [(a, 2)],
            [(m, 1)],
            [(m, 2), (a, 3)],
            [(r, 1)],
            [(m, 3)],
            [(r, 2), (s, (0, 1))],
            [(r, 3)],
            [(s, (2,))],
            [(s, (3,))],
        ], [(0, 1), (2,), (3,)]
    slots = [[(m, 0)]]
    for d in range(1, nz):
        slots.append([(a, d)] + ([(f, d)] if d & -d > 1 else []))
        slots.append([(m, d), (r, d - 1)])
    slots += [[(r, nz - 1)]] + [[(s, (d,))] for d in range(nz)]
    return slots, [(d,) for d in range(nz)]


def solution(mesh):
    holders, pairs = mesh.shape["blk"], mesh.shape["pair"]
    nx = 1
    while (2 * nx) ** 2 <= holders:
        nx *= 2
    nc = 2 if pairs % 2 == 0 else 1
    placed = (
        P("pair", "blk", None, None),
        P("pair", "blk", None),
        P("blk", "pair", None),
        P("blk", None),
        P("blk"),
        P(),
    )
    return jax.shard_map(
        functools.partial(per_device, holders // nx, nx, pairs // nc, nc),
        mesh=mesh,
        in_specs=placed,
        out_specs=P("blk", "pair", None, None),
        check_vma=False,
    )
```

```python
import functools

import jax
import jax.numpy as jnp
from jax import lax
from jax.experimental import pallas as pl
from jax.experimental.pallas import tpu as pltpu
from jax.sharding import PartitionSpec as P

LANES = 128
SMEM = pl.BlockSpec(memory_space=pltpu.SMEM)
VMEM = pl.BlockSpec(memory_space=pltpu.VMEM)
ANY = pl.BlockSpec(memory_space=pl.ANY)
GRANT = 32 * 2**20
PACE = 0.3e9


def blk_swap(value, dz, dx, nz, nx):
    pairs = [(z * nx + x, (z ^ dz) * nx + (x ^ dx)) for z in range(nz) for x in range(nx)]
    return lax.ppermute(value, "blk", pairs)


def slab_swap(value, dx, dy, nz, nx, ny, nc):
    pairs = [
        (((z * nx + x) * ny + y) * nc + c, ((z * nx + (x ^ dx)) * ny + (y ^ dy)) * nc + c)
        for z in range(nz)
        for x in range(nx)
        for y in range(ny)
        for c in range(nc)
    ]
    return lax.ppermute(value, ("blk", "pair"), pairs)


def pair_swap(value, dy, dc, ny, nc):
    pairs = [(y * nc + c, (y ^ dy) * nc + (c ^ dc)) for y in range(ny) for c in range(nc)]
    return lax.ppermute(value, "pair", pairs)


def pick(position, options):
    value = options[0]
    for index in range(1, len(options)):
        value = jnp.where(position == index, options[index], value)
    return value


def bf16(*shape):
    return jax.ShapeDtypeStruct(shape, jnp.bfloat16)


class Step:
    def __init__(self, body, scalars, arrays, outs, scratch=(), far=()):
        self.body, self.scalars, self.arrays, self.far = body, list(scalars), list(arrays), list(far)
        self.outs, self.scratch = list(outs), list(scratch)


def launch(name, steps, after, due):
    scalars, arrays = [], []
    far = [value for step in steps for value in step.far]
    for step in steps:
        for value in step.scalars:
            if not any(value is other for other in scalars):
                scalars.append(value)
        for value in step.arrays:
            if not any(value is other for other in arrays):
                arrays.append(value)
    operands = scalars + arrays + far
    find = lambda value: next(i for i, other in enumerate(operands) if other is value)
    outs = [out for step in steps for out in step.outs]
    scratch = [s for step in steps for s in step.scratch]

    def kernel(*refs):
        out_refs = refs[len(operands) + len(after) :]
        scratch_refs = out_refs[len(outs) :]
        o = s = 0
        for step in steps:
            step.body(
                [refs[find(value)] for value in step.scalars],
                [refs[find(value)] for value in step.arrays + step.far],
                out_refs[o : o + len(step.outs)],
                scratch_refs[s : s + len(step.scratch)],
            )
            o, s = o + len(step.outs), s + len(step.scratch)

    results = pl.pallas_call(
        kernel,
        in_specs=[SMEM] * len(scalars) + [VMEM] * len(arrays) + [ANY] * (len(far) + len(after)),
        out_specs=[VMEM] * len(outs),
        out_shape=outs,
        scratch_shapes=scratch,
        cost_estimate=pl.CostEstimate(flops=int(PACE * due), bytes_accessed=0, transcendentals=0),
        compiler_params=pltpu.CompilerParams(vmem_limit_bytes=GRANT),
        name=name,
    )(*operands, *after)
    split, o = [], 0
    for step in steps:
        split.append(results[o : o + len(step.outs)])
        o += len(step.outs)
    return split


class Rows:
    def __init__(self, arrays, packed):
        self.arrays, self.packed = list(arrays), packed


def gather_rows(refs, index):
    return jnp.concatenate([ref[index] for ref in refs], axis=0) if len(refs) > 1 else refs[0][index]


def read_codes(ref, slots):
    row = ref[ref.shape[0] - 1][:1].astype(jnp.float32)
    lane = lax.broadcasted_iota(jnp.int32, row.shape, 1)
    return [jnp.sum(jnp.where(lane == k, row, 0.0)).astype(jnp.int32) for k in range(slots)]


def pack(codes, rows, slots):
    total = sum(value.shape[1] for value in rows.arrays)

    def body(_, refs, outs, __):
        for k, tile in enumerate(read_codes(refs[-1], slots)):
            outs[0][k] = gather_rows(refs[:-1], tile)

    return Step(body, [], [*rows.arrays, codes], [bf16(slots, total, rows.arrays[0].shape[2])])


def through(arrays):
    tiles, _, depth = arrays[0].shape

    def body(_, refs, outs, __):
        outs[0][...] = jnp.concatenate([ref[...] for ref in refs], axis=1) if len(refs) > 1 else refs[0][...]

    return Step(body, [], arrays, [bf16(tiles, sum(value.shape[1] for value in arrays), depth)])


def hold(value):
    def body(_, refs, outs, scratch):
        copy = pltpu.make_async_copy(refs[0], outs[0], scratch[0])
        copy.start()
        copy.wait()

    return Step(body, [], [], [bf16(*value.shape)], [pltpu.SemaphoreType.DMA(())], [value])


def products(codes, sources, blocks, ny, rows):
    nx, nc = len(sources), len(blocks)
    slots, depth, width = blocks[0].shape
    counts = [len(source.arrays) for source in sources]
    starts = [sum(counts[:d]) for d in range(nx + 1)]

    def body(_, refs, outs, __):
        block_refs = refs[starts[-1] : -1]
        x, c = lax.axis_index("blk") % nx, lax.axis_index("pair") % nc
        for k, tile in enumerate(read_codes(refs[-1], slots)):
            parts = [gather_rows(refs[starts[d] : starts[d + 1]], k if sources[d].packed else tile) for d in range(nx)]
            parts = [pick(x ^ i, parts) for i in range(nx)]
            columns = []
            for part in range(nc):
                pieces = [p[(s * nc + part) * rows : (s * nc + part + 1) * rows] for p in parts for s in range(ny)]
                columns.append(jnp.concatenate(pieces, axis=0))
            total = None
            for d in range(nc):
                term = jnp.dot(pick(c ^ d, columns), block_refs[d][k], preferred_element_type=jnp.float32)
                total = term if total is None else total + term
            for s in range(ny):
                pieces = [total[(i * ny + s) * rows : (i * ny + s + 1) * rows] for i in range(nx)]
                outs[s][k] = jnp.concatenate(pieces, axis=0).astype(outs[s].dtype)

    arrays = [value for source in sources for value in source.arrays] + [*blocks, codes]
    return Step(body, [], arrays, [bf16(slots, nx * rows, width)] * ny)


def route(tiles, keep, slot_tile, parts, tile_count, nx, nz):
    slots, rows, width = parts[0].shape
    owned = slot_tile.shape[0] // (nx * nz)
    per_tile = width // LANES

    def body(scalars, refs, outs, scratch):
        tiles_ref, keep_ref, slot_ref = scalars
        total = scratch[0]
        z, x = lax.axis_index("blk") // nx, lax.axis_index("blk") % nx
        total[...] = jnp.zeros_like(total)

        def add(k, _):
            value = refs[0][k].astype(jnp.float32)
            for ref in refs[1:]:
                value += ref[k].astype(jnp.float32)
            total[tiles_ref[1, k]] += value * keep_ref[k].astype(jnp.float32)
            return 0

        lax.fori_loop(0, slots, add, 0)
        for d in range(nx):
            for dz in range(nz):
                owner = (z ^ dz) * nx + (x ^ d)
                for i in range(owned):
                    tile = slot_ref[owner * owned + i]
                    a = lax.div(tile, per_tile)
                    column = pl.multiple_of(lax.rem(tile, per_tile) * LANES, LANES)
                    outs[d][dz * owned + i] = total[a, :, pl.ds(column, LANES)].astype(outs[d].dtype)

    scratch = [pltpu.VMEM((tile_count, rows, width), jnp.float32)]
    return Step(body, [tiles, keep, slot_tile], parts, [bf16(nz * owned, rows, LANES)] * nx, scratch)


def add_split(chunks, nz):
    tiles, rows, lanes = chunks[0][0].shape
    count, each = tiles // nz, len(chunks[0])

    def body(_, refs, outs, __):
        for i in range(len(chunks)):
            for e, out in enumerate(outs):
                span = slice(e * count, (e + 1) * count)
                value = refs[i * each][span].astype(jnp.float32)
                for part in refs[i * each + 1 : (i + 1) * each]:
                    value += part[span].astype(jnp.float32)
                out[:, i] = value.astype(out.dtype)

    flat = [part for chunk in chunks for part in chunk]
    return Step(body, [], flat, [bf16(count, len(chunks), rows, lanes)] * nz)


def fold(chunks, nz):
    tiles, rows, lanes = chunks[0][0].shape
    count, each = tiles // nz, len(chunks[0])

    def body(_, refs, outs, __):
        for i in range(len(chunks)):
            for e in range(nz):
                span = slice(e * count, (e + 1) * count)
                value = refs[i * each][span].astype(jnp.float32)
                for part in refs[i * each + 1 : (i + 1) * each]:
                    value += part[span].astype(jnp.float32)
                at = slice(e // 2 * count, (e // 2 + 1) * count)
                outs[e % 2][at, i ^ e % 2] = value.astype(outs[e % 2].dtype)

    flat = [part for chunk in chunks for part in chunk]
    return Step(body, [], flat, [bf16(nz // 2 * count, len(chunks), rows, lanes)] * 2)


def final_sum(received, nz, nx):
    owned, _, rows, lanes = received[0][0].shape

    def body(scalars, refs, outs, _):
        z = lax.axis_index("blk") // nx
        for ahead in range(nz):
            value = None
            for ref, (_, columns) in zip(refs, received, strict=True):
                if ahead in columns:
                    term = ref[:, columns.index(ahead)].astype(jnp.float32)
                    value = term if value is None else value + term
            outs[0][:, z ^ ahead] = value.astype(outs[0].dtype)

    return Step(body, [], [value for value, _ in received], [bf16(owned, nz, rows, lanes)])


def per_device(nz, nx, ny, nc, amplitudes, tile_mask, integrals, block_tiles, block_keep, slot_tile):
    pair = lax.axis_index("pair")
    y = pair // nc
    _, rows, tile_count, contracted = amplitudes.shape
    slots = block_keep.shape[0]
    columns = contracted // ny

    siblings = [pair_swap(integrals, 0, d, ny, nc) for d in range(1, nc)]
    blocks = [integrals]
    tiles = block_tiles.T

    masked = jnp.where(tile_mask[0][:, :, None] != 0, amplitudes[0], jnp.zeros((), amplitudes.dtype))
    masked = masked.transpose(1, 0, 2)
    depth = columns // nc
    pieces = []
    for d in range(ny):
        begin = (y ^ d) * columns
        pieces.append(
            jnp.concatenate([lax.dynamic_slice_in_dim(masked, begin + i * depth, depth, axis=2) for i in range(nc)], axis=1)
        )

    here, others, partial, by_owner, folded, received = {}, {}, {}, {}, {}, []
    last = []

    def run(name, due, *steps):
        nonlocal last
        results = launch(name, [step for step, _ in steps], last, due)
        last = list(results[0][:1])
        for (_, use), result in zip(steps, results, strict=True):
            use(result)

    def low_bits():
        return [d for d in range(1, nz) if d & -d == d]

    def do_first(s):
        def use(out):
            for d in range(1, nx):
                others[0][d - 1].append(blk_swap(out[0], 0, d, nz, nx))

        return through([from_y[s]]), use

    def do_along():
        def use(out):
            for d in low_bits():
                here[d] = [blk_swap(out[0], d, 0, nz, nx)]

        return through(from_y), use

    def do_hold(i):
        return hold(siblings[i]), lambda out: blocks.append(out[0])

    def do_pack(d, i):
        def use(out):
            if i:
                others[d][i] = blk_swap(out[0], 0, i, nz, nx)
            else:
                own[d] = out[0]

        others.setdefault(d, {})
        if i:
            return pack(their_codes[i - 1], Rows(here[d], False), slots), use
        return pack(first, Rows(here[d], False), slots), use

    def do_forward(d):
        def use(out):
            for step in range(1, d & -d):
                if step & -step == step:
                    here[d | step] = [blk_swap(out[0], step, 0, nz, nx)]

        return through(here[d]), use

    def do_products(d):
        def use(out):
            partial[d] = [out[0]] + [pair_swap(out[i], i, 0, ny, nc) for i in range(1, ny)]

        if d:
            sources = [Rows([own[d]], True) if d in own else Rows(here[d], False)]
            sources += [Rows([others[d][i]], True) for i in range(1, nx)]
        else:
            sources = [Rows(from_y, False)] + [Rows(other, False) for other in others[0]]
        return products(first, sources, blocks, ny, rows), use

    def do_route(d):
        def use(out):
            by_owner[d] = [out[0]] + [blk_swap(out[i], 0, i, nz, nx) for i in range(1, nx)]

        return route(tiles, block_keep, slot_tile, partial[d], tile_count, nx, nz), use

    def do_add(group):
        def use(out):
            for e in range(nz):
                received.append((blk_swap(out[e], e, 0, nz, nx) if e else out[0], [e ^ d for d in group]))

        return add_split([by_owner[d] for d in group], nz), use

    def do_fold(group):
        def use(out):
            folded[group] = [out[0], blk_swap(out[1], 1, 0, nz, nx)]

        return fold([by_owner[d] for d in group], nz), use

    def do_pass(group):
        def use(out):
            for e in range(0, nz, 2):
                received.append((blk_swap(out[e // 2], e, 0, nz, nx) if e else out[0], [e ^ d for d in group]))

        chunks = [[value.reshape(value.shape[0], -1, LANES) for value in folded[group]]]
        step = add_split(chunks, nz // 2)
        return step, lambda out: use([value.reshape(value.shape[0], len(group), -1, LANES) for value in out])

    from_y = [pieces[0]] + [pair_swap(pieces[d], d, 0, ny, nc) for d in range(1, ny)]
    codes = jnp.pad(tiles[:1].astype(jnp.bfloat16), ((0, nc * rows - 1), (0, depth - slots)))
    first = jnp.concatenate([pieces[0], codes[None]], axis=0)
    others[0] = [[blk_swap(first, 0, dx, nz, nx)] for dx in range(1, nx)]
    their_codes = [other[0] for other in others[0]]
    own = {}
    if nc > 1:
        run("hold", 8, *[do_hold(i) for i in range(nc - 1)])
    run("first", 20, *[do_first(s) for s in range(1, ny)], do_along())
    for due, slot in plan(nz):
        steps = []
        last = last + [value for what, g in slot if what == "sent" for value, _ in received[g * nz : (g + 1) * nz]]
        last = last + [value for what, d in slot if what == "came" for value in here[d]]
        last = last + [value for what, d in slot if what == "got" for value in partial[d][1:]]
        for what, d in slot:
            if what == "arrive":
                steps += [do_pack(d, i) for i in range(1, nx)] + ([do_pack(d, 0)] if len(here[d]) > 1 else [])
            elif what == "forward":
                steps.append(do_forward(d))
            elif what not in ("sent", "came", "got"):
                steps.append({"multiply": do_products, "route": do_route, "add": do_add, "fold": do_fold, "pass": do_pass}[what](d))
        run("_".join(what for what, _ in slot), due, *steps)
    out = launch("final_sum", [final_sum(received, nz, nx)], last, 2)[0][0]
    return out.reshape(out.shape[0], 1, out.shape[1] * out.shape[2], LANES)


def plan(nz):
    m, r, a, f, s = "multiply", "route", "arrive", "forward", "add"
    if nz == 4:
        return [
            (2, [(m, 0)]),
            (4, [(a, 1)]),
            (6, [(f, 2)]),
            (20, [(r, 0)]),
            (20, [(a, 2)]),
            (20, [(m, 1)]),
            (20, [(m, 2), (a, 3)]),
            (20, [(s, (0,))]),
            (20, [(r, 1)]),
            (20, [(m, 3), ("sent", 0)]),
            (20, [(r, 2)]),
            (20, [(s, (1,))]),
            (20, [(r, 3)]),
            (20, [(s, (2,))]),
            (20, [(s, (3,)), ("sent", 1)]),
        ]
    slots = [[(m, 0)]]
    for d in range(1, nz):
        slots.append([(a, d)] + ([(f, d)] if d & -d > 1 else []))
        slots.append([(m, d), (r, d - 1)])
    slots += [[(r, nz - 1)]] + [[(s, (d,))] for d in range(nz)]
    return [(5.0, slot) for slot in slots]


def solution(mesh):
    holders, pairs = mesh.shape["blk"], mesh.shape["pair"]
    nx = 1
    while (2 * nx) ** 2 <= holders:
        nx *= 2
    nc = 2 if pairs % 2 == 0 else 1
    placed = (
        P("pair", "blk", None, None),
        P("pair", "blk", None),
        P("blk", "pair", None),
        P("blk", None),
        P("blk"),
        P(),
    )
    return jax.shard_map(
        functools.partial(per_device, holders // nx, nx, pairs // nc, nc),
        mesh=mesh,
        in_specs=placed,
        out_specs=P("blk", "pair", None, None),
        check_vma=False,
    )
```

```python
import functools

import jax
import jax.numpy as jnp
from jax import lax
from jax.experimental import pallas as pl
from jax.experimental.pallas import tpu as pltpu
from jax.sharding import PartitionSpec as P

LANES = 128
SMEM = pl.BlockSpec(memory_space=pltpu.SMEM)
VMEM = pl.BlockSpec(memory_space=pltpu.VMEM)
ANY = pl.BlockSpec(memory_space=pl.ANY)
GRANT = 32 * 2**20
PACE = 0.3e9


def blk_swap(value, dz, dx, nz, nx):
    pairs = [(z * nx + x, (z ^ dz) * nx + (x ^ dx)) for z in range(nz) for x in range(nx)]
    return lax.ppermute(value, "blk", pairs)


def slab_swap(value, dx, dy, nz, nx, ny, nc):
    pairs = [
        (((z * nx + x) * ny + y) * nc + c, ((z * nx + (x ^ dx)) * ny + (y ^ dy)) * nc + c)
        for z in range(nz)
        for x in range(nx)
        for y in range(ny)
        for c in range(nc)
    ]
    return lax.ppermute(value, ("blk", "pair"), pairs)


def pair_swap(value, dy, dc, ny, nc):
    pairs = [(y * nc + c, (y ^ dy) * nc + (c ^ dc)) for y in range(ny) for c in range(nc)]
    return lax.ppermute(value, "pair", pairs)


def pick(position, options):
    value = options[0]
    for index in range(1, len(options)):
        value = jnp.where(position == index, options[index], value)
    return value


def bf16(*shape):
    return jax.ShapeDtypeStruct(shape, jnp.bfloat16)


class Step:
    def __init__(self, body, scalars, arrays, outs, scratch=(), far=()):
        self.body, self.scalars, self.arrays, self.far = body, list(scalars), list(arrays), list(far)
        self.outs, self.scratch = list(outs), list(scratch)


def launch(name, steps, after, due):
    scalars, arrays = [], []
    far = [value for step in steps for value in step.far]
    for step in steps:
        for value in step.scalars:
            if not any(value is other for other in scalars):
                scalars.append(value)
        for value in step.arrays:
            if not any(value is other for other in arrays):
                arrays.append(value)
    operands = scalars + arrays + far
    find = lambda value: next(i for i, other in enumerate(operands) if other is value)
    outs = [out for step in steps for out in step.outs]
    scratch = [s for step in steps for s in step.scratch]

    def kernel(*refs):
        out_refs = refs[len(operands) + len(after) :]
        scratch_refs = out_refs[len(outs) :]
        o = s = 0
        for step in steps:
            step.body(
                [refs[find(value)] for value in step.scalars],
                [refs[find(value)] for value in step.arrays + step.far],
                out_refs[o : o + len(step.outs)],
                scratch_refs[s : s + len(step.scratch)],
            )
            o, s = o + len(step.outs), s + len(step.scratch)

    results = pl.pallas_call(
        kernel,
        in_specs=[SMEM] * len(scalars) + [VMEM] * len(arrays) + [ANY] * (len(far) + len(after)),
        out_specs=[VMEM] * len(outs),
        out_shape=outs,
        scratch_shapes=scratch,
        cost_estimate=pl.CostEstimate(flops=int(PACE * due), bytes_accessed=0, transcendentals=0),
        compiler_params=pltpu.CompilerParams(vmem_limit_bytes=GRANT),
        name=name,
    )(*operands, *after)
    split, o = [], 0
    for step in steps:
        split.append(results[o : o + len(step.outs)])
        o += len(step.outs)
    return split


class Rows:
    def __init__(self, arrays, packed):
        self.arrays, self.packed = list(arrays), packed


def gather_rows(refs, index):
    return jnp.concatenate([ref[index] for ref in refs], axis=0) if len(refs) > 1 else refs[0][index]


def read_codes(ref, slots):
    row = ref[ref.shape[0] - 1][:1].astype(jnp.float32)
    lane = lax.broadcasted_iota(jnp.int32, row.shape, 1)
    return [jnp.sum(jnp.where(lane == k, row, 0.0)).astype(jnp.int32) for k in range(slots)]


def pack(codes, rows, slots):
    total = sum(value.shape[1] for value in rows.arrays)

    def body(_, refs, outs, __):
        for k, tile in enumerate(read_codes(refs[-1], slots)):
            outs[0][k] = gather_rows(refs[:-1], tile)

    return Step(body, [], [*rows.arrays, codes], [bf16(slots, total, rows.arrays[0].shape[2])])


def through(arrays):
    tiles, _, depth = arrays[0].shape

    def body(_, refs, outs, __):
        outs[0][...] = jnp.concatenate([ref[...] for ref in refs], axis=1) if len(refs) > 1 else refs[0][...]

    return Step(body, [], arrays, [bf16(tiles, sum(value.shape[1] for value in arrays), depth)])


def hold(value):
    def body(_, refs, outs, scratch):
        copy = pltpu.make_async_copy(refs[0], outs[0], scratch[0])
        copy.start()
        copy.wait()

    return Step(body, [], [], [bf16(*value.shape)], [pltpu.SemaphoreType.DMA(())], [value])


def products(codes, sources, blocks, ny, rows):
    nx, nc = len(sources), len(blocks)
    slots, depth, width = blocks[0].shape
    counts = [len(source.arrays) for source in sources]
    starts = [sum(counts[:d]) for d in range(nx + 1)]

    def body(_, refs, outs, __):
        block_refs = refs[starts[-1] : -1]
        x, c = lax.axis_index("blk") % nx, lax.axis_index("pair") % nc
        for k, tile in enumerate(read_codes(refs[-1], slots)):
            parts = [gather_rows(refs[starts[d] : starts[d + 1]], k if sources[d].packed else tile) for d in range(nx)]
            parts = [pick(x ^ i, parts) for i in range(nx)]
            columns = []
            for part in range(nc):
                pieces = [p[(s * nc + part) * rows : (s * nc + part + 1) * rows] for p in parts for s in range(ny)]
                columns.append(jnp.concatenate(pieces, axis=0))
            total = None
            for d in range(nc):
                term = jnp.dot(pick(c ^ d, columns), block_refs[d][k], preferred_element_type=jnp.float32)
                total = term if total is None else total + term
            for s in range(ny):
                pieces = [total[(i * ny + s) * rows : (i * ny + s + 1) * rows] for i in range(nx)]
                outs[s][k] = jnp.concatenate(pieces, axis=0).astype(outs[s].dtype)

    arrays = [value for source in sources for value in source.arrays] + [*blocks, codes]
    return Step(body, [], arrays, [bf16(slots, nx * rows, width)] * ny)


def route(tiles, keep, slot_tile, parts, tile_count, nx, nz):
    slots, rows, width = parts[0].shape
    owned = slot_tile.shape[0] // (nx * nz)
    per_tile = width // LANES

    def body(scalars, refs, outs, scratch):
        tiles_ref, keep_ref, slot_ref = scalars
        total = scratch[0]
        z, x = lax.axis_index("blk") // nx, lax.axis_index("blk") % nx
        total[...] = jnp.zeros_like(total)

        def add(k, _):
            value = refs[0][k].astype(jnp.float32)
            for ref in refs[1:]:
                value += ref[k].astype(jnp.float32)
            total[tiles_ref[1, k]] += value * keep_ref[k].astype(jnp.float32)
            return 0

        lax.fori_loop(0, slots, add, 0)
        for d in range(nx):
            for dz in range(nz):
                owner = (z ^ dz) * nx + (x ^ d)
                for i in range(owned):
                    tile = slot_ref[owner * owned + i]
                    a = lax.div(tile, per_tile)
                    column = pl.multiple_of(lax.rem(tile, per_tile) * LANES, LANES)
                    outs[d][dz * owned + i] = total[a, :, pl.ds(column, LANES)].astype(outs[d].dtype)

    scratch = [pltpu.VMEM((tile_count, rows, width), jnp.float32)]
    return Step(body, [tiles, keep, slot_tile], parts, [bf16(nz * owned, rows, LANES)] * nx, scratch)


def add_split(chunks, nz):
    tiles, rows, lanes = chunks[0][0].shape
    count, each = tiles // nz, len(chunks[0])

    def body(_, refs, outs, __):
        for i in range(len(chunks)):
            for e, out in enumerate(outs):
                span = slice(e * count, (e + 1) * count)
                value = refs[i * each][span].astype(jnp.float32)
                for part in refs[i * each + 1 : (i + 1) * each]:
                    value += part[span].astype(jnp.float32)
                out[:, i] = value.astype(out.dtype)

    flat = [part for chunk in chunks for part in chunk]
    return Step(body, [], flat, [bf16(count, len(chunks), rows, lanes)] * nz)


def fold(chunks, nz):
    tiles, rows, lanes = chunks[0][0].shape
    count, each = tiles // nz, len(chunks[0])

    def body(_, refs, outs, __):
        for i in range(len(chunks)):
            for e in range(nz):
                span = slice(e * count, (e + 1) * count)
                value = refs[i * each][span].astype(jnp.float32)
                for part in refs[i * each + 1 : (i + 1) * each]:
                    value += part[span].astype(jnp.float32)
                at = slice(e // 2 * count, (e // 2 + 1) * count)
                outs[e % 2][at, i ^ e % 2] = value.astype(outs[e % 2].dtype)

    flat = [part for chunk in chunks for part in chunk]
    return Step(body, [], flat, [bf16(nz // 2 * count, len(chunks), rows, lanes)] * 2)


def final_sum(received, nz, nx):
    owned, _, rows, lanes = received[0][0].shape

    def body(scalars, refs, outs, _):
        z = lax.axis_index("blk") // nx
        for ahead in range(nz):
            value = None
            for ref, (_, columns) in zip(refs, received, strict=True):
                if ahead in columns:
                    term = ref[:, columns.index(ahead)].astype(jnp.float32)
                    value = term if value is None else value + term
            outs[0][:, z ^ ahead] = value.astype(outs[0].dtype)

    return Step(body, [], [value for value, _ in received], [bf16(owned, nz, rows, lanes)])


def per_device(nz, nx, ny, nc, amplitudes, tile_mask, integrals, block_tiles, block_keep, slot_tile):
    pair = lax.axis_index("pair")
    y = pair // nc
    _, rows, tile_count, contracted = amplitudes.shape
    slots = block_keep.shape[0]
    columns = contracted // ny

    siblings = [pair_swap(integrals, 0, d, ny, nc) for d in range(1, nc)]
    blocks = [integrals]
    tiles = block_tiles.T

    masked = jnp.where(tile_mask[0][:, :, None] != 0, amplitudes[0], jnp.zeros((), amplitudes.dtype))
    masked = masked.transpose(1, 0, 2)
    depth = columns // nc
    pieces = []
    for d in range(ny):
        begin = (y ^ d) * columns
        pieces.append(
            jnp.concatenate([lax.dynamic_slice_in_dim(masked, begin + i * depth, depth, axis=2) for i in range(nc)], axis=1)
        )

    here, others, partial, by_owner, folded, received = {}, {}, {}, {}, {}, []
    last = []

    def run(name, due, *steps):
        nonlocal last
        results = launch(name, [step for step, _ in steps], last, due)
        last = list(results[0][:1])
        for (_, use), result in zip(steps, results, strict=True):
            use(result)

    def low_bits():
        return [d for d in range(1, nz) if d & -d == d]

    def do_first(s):
        def use(out):
            for d in range(1, nx):
                others[0][d - 1].append(blk_swap(out[0], 0, d, nz, nx))

        return through([from_y[s]]), use

    def do_along():
        def use(out):
            for d in low_bits():
                here[d] = [blk_swap(out[0], d, 0, nz, nx)]

        return through(from_y), use

    def do_hold(i):
        return hold(siblings[i]), lambda out: blocks.append(out[0])

    def do_pack(d, i):
        def use(out):
            if i:
                others[d][i] = blk_swap(out[0], 0, i, nz, nx)
            else:
                own[d] = out[0]

        others.setdefault(d, {})
        if i:
            return pack(their_codes[i - 1], Rows(here[d], False), slots), use
        return pack(first, Rows(here[d], False), slots), use

    def do_forward(d):
        def use(out):
            for step in range(1, d & -d):
                if step & -step == step:
                    here[d | step] = [blk_swap(out[0], step, 0, nz, nx)]

        return through(here[d]), use

    def do_products(d):
        def use(out):
            partial[d] = [out[0]] + [pair_swap(out[i], i, 0, ny, nc) for i in range(1, ny)]

        if d:
            sources = [Rows([own[d]], True) if d in own else Rows(here[d], False)]
            sources += [Rows([others[d][i]], True) for i in range(1, nx)]
        else:
            sources = [Rows(from_y, False)] + [Rows(other, False) for other in others[0]]
        return products(first, sources, blocks, ny, rows), use

    def do_route(d):
        def use(out):
            by_owner[d] = [out[0]] + [blk_swap(out[i], 0, i, nz, nx) for i in range(1, nx)]

        return route(tiles, block_keep, slot_tile, partial[d], tile_count, nx, nz), use

    def do_add(group):
        def use(out):
            for e in reversed(range(nz)):
                received.append((blk_swap(out[e], e, 0, nz, nx) if e else out[0], [e ^ d for d in group]))

        return add_split([by_owner[d] for d in group], nz), use

    def do_fold(group):
        def use(out):
            folded[group] = [out[0], blk_swap(out[1], 1, 0, nz, nx)]

        return fold([by_owner[d] for d in group], nz), use

    def do_pass(group):
        def use(out):
            for e in range(0, nz, 2):
                received.append((blk_swap(out[e // 2], e, 0, nz, nx) if e else out[0], [e ^ d for d in group]))

        chunks = [[value.reshape(value.shape[0], -1, LANES) for value in folded[group]]]
        step = add_split(chunks, nz // 2)
        return step, lambda out: use([value.reshape(value.shape[0], len(group), -1, LANES) for value in out])

    from_y = [pieces[0]] + [pair_swap(pieces[d], d, 0, ny, nc) for d in range(1, ny)]
    codes = jnp.pad(tiles[:1].astype(jnp.bfloat16), ((0, nc * rows - 1), (0, depth - slots)))
    first = jnp.concatenate([pieces[0], codes[None]], axis=0)
    others[0] = [[blk_swap(first, 0, dx, nz, nx)] for dx in range(1, nx)]
    their_codes = [other[0] for other in others[0]]
    own = {}
    if nc > 1:
        run("hold", 8, *[do_hold(i) for i in range(nc - 1)])
    run("first", 20, *[do_first(s) for s in range(1, ny)], do_along())
    for due, slot in plan(nz):
        steps = []
        last = last + [value for what, g in slot if what == "sent" for value, _ in received[g * nz : (g + 1) * nz]]
        last = last + [value for what, d in slot if what == "came" for value in here[d]]
        last = last + [value for what, d in slot if what == "got" for value in partial[d][1:]]
        for what, d in slot:
            if what == "arrive":
                steps += [do_pack(d, i) for i in range(1, nx)] + ([do_pack(d, 0)] if len(here[d]) > 1 else [])
            elif what == "forward":
                steps.append(do_forward(d))
            elif what not in ("sent", "came", "got"):
                steps.append({"multiply": do_products, "route": do_route, "add": do_add, "fold": do_fold, "pass": do_pass}[what](d))
        run("_".join(what for what, _ in slot), due, *steps)
    out = launch("final_sum", [final_sum(received, nz, nx)], last, 2)[0][0]
    return out.reshape(out.shape[0], 1, out.shape[1] * out.shape[2], LANES)


def plan(nz):
    m, r, a, f, s = "multiply", "route", "arrive", "forward", "add"
    if nz == 4:
        return [
            (2, [(m, 0)]),
            (4, [(a, 1)]),
            (6, [(f, 2)]),
            (20, [(r, 0)]),
            (20, [(a, 2)]),
            (20, [(m, 1)]),
            (20, [(m, 2), (a, 3)]),
            (20, [(s, (0,))]),
            (20, [(r, 1)]),
            (20, [(m, 3)]),
            (20, [(r, 2), ("sent", 0)]),
            (20, [(s, (1,))]),
            (20, [(r, 3)]),
            (20, [(s, (2,))]),
            (20, [(s, (3,)), ("sent", 1)]),
        ]
    slots = [[(m, 0)]]
    for d in range(1, nz):
        slots.append([(a, d)] + ([(f, d)] if d & -d > 1 else []))
        slots.append([(m, d), (r, d - 1)])
    slots += [[(r, nz - 1)]] + [[(s, (d,))] for d in range(nz)]
    return [(5.0, slot) for slot in slots]


def solution(mesh):
    holders, pairs = mesh.shape["blk"], mesh.shape["pair"]
    nx = 1
    while (2 * nx) ** 2 <= holders:
        nx *= 2
    nc = 2 if pairs % 2 == 0 else 1
    placed = (
        P("pair", "blk", None, None),
        P("pair", "blk", None),
        P("blk", "pair", None),
        P("blk", None),
        P("blk"),
        P(),
    )
    return jax.shard_map(
        functools.partial(per_device, holders // nx, nx, pairs // nc, nc),
        mesh=mesh,
        in_specs=placed,
        out_specs=P("blk", "pair", None, None),
        check_vma=False,
    )
```

```python
import functools

import jax
import jax.numpy as jnp
from jax import lax
from jax.experimental import pallas as pl
from jax.experimental.pallas import tpu as pltpu
from jax.sharding import PartitionSpec as P

LANES = 128
SMEM = pl.BlockSpec(memory_space=pltpu.SMEM)
VMEM = pl.BlockSpec(memory_space=pltpu.VMEM)
ANY = pl.BlockSpec(memory_space=pl.ANY)
GRANT = 32 * 2**20
PACE = 0.3e9


def blk_swap(value, dz, dx, nz, nx):
    pairs = [(z * nx + x, (z ^ dz) * nx + (x ^ dx)) for z in range(nz) for x in range(nx)]
    return lax.ppermute(value, "blk", pairs)


def slab_swap(value, dx, dy, nz, nx, ny, nc):
    pairs = [
        (((z * nx + x) * ny + y) * nc + c, ((z * nx + (x ^ dx)) * ny + (y ^ dy)) * nc + c)
        for z in range(nz)
        for x in range(nx)
        for y in range(ny)
        for c in range(nc)
    ]
    return lax.ppermute(value, ("blk", "pair"), pairs)


def pair_swap(value, dy, dc, ny, nc):
    pairs = [(y * nc + c, (y ^ dy) * nc + (c ^ dc)) for y in range(ny) for c in range(nc)]
    return lax.ppermute(value, "pair", pairs)


def pick(position, options):
    value = options[0]
    for index in range(1, len(options)):
        value = jnp.where(position == index, options[index], value)
    return value


def bf16(*shape):
    return jax.ShapeDtypeStruct(shape, jnp.bfloat16)


class Step:
    def __init__(self, body, scalars, arrays, outs, scratch=(), far=()):
        self.body, self.scalars, self.arrays, self.far = body, list(scalars), list(arrays), list(far)
        self.outs, self.scratch = list(outs), list(scratch)


def launch(name, steps, after, due):
    scalars, arrays = [], []
    far = [value for step in steps for value in step.far]
    for step in steps:
        for value in step.scalars:
            if not any(value is other for other in scalars):
                scalars.append(value)
        for value in step.arrays:
            if not any(value is other for other in arrays):
                arrays.append(value)
    operands = scalars + arrays + far
    find = lambda value: next(i for i, other in enumerate(operands) if other is value)
    outs = [out for step in steps for out in step.outs]
    scratch = [s for step in steps for s in step.scratch]

    def kernel(*refs):
        out_refs = refs[len(operands) + len(after) :]
        scratch_refs = out_refs[len(outs) :]
        o = s = 0
        for step in steps:
            step.body(
                [refs[find(value)] for value in step.scalars],
                [refs[find(value)] for value in step.arrays + step.far],
                out_refs[o : o + len(step.outs)],
                scratch_refs[s : s + len(step.scratch)],
            )
            o, s = o + len(step.outs), s + len(step.scratch)

    results = pl.pallas_call(
        kernel,
        in_specs=[SMEM] * len(scalars) + [VMEM] * len(arrays) + [ANY] * (len(far) + len(after)),
        out_specs=[VMEM] * len(outs),
        out_shape=outs,
        scratch_shapes=scratch,
        cost_estimate=pl.CostEstimate(flops=int(PACE * due), bytes_accessed=0, transcendentals=0),
        compiler_params=pltpu.CompilerParams(vmem_limit_bytes=GRANT),
        name=name,
    )(*operands, *after)
    split, o = [], 0
    for step in steps:
        split.append(results[o : o + len(step.outs)])
        o += len(step.outs)
    return split


class Rows:
    def __init__(self, arrays, packed):
        self.arrays, self.packed = list(arrays), packed


def gather_rows(refs, index):
    return jnp.concatenate([ref[index] for ref in refs], axis=0) if len(refs) > 1 else refs[0][index]


def read_codes(ref, slots):
    row = ref[ref.shape[0] - 1][:1].astype(jnp.float32)
    lane = lax.broadcasted_iota(jnp.int32, row.shape, 1)
    return [jnp.sum(jnp.where(lane == k, row, 0.0)).astype(jnp.int32) for k in range(slots)]


def pack(codes, rows, slots):
    total = sum(value.shape[1] for value in rows.arrays)

    def body(_, refs, outs, __):
        for k, tile in enumerate(read_codes(refs[-1], slots)):
            outs[0][k] = gather_rows(refs[:-1], tile)

    return Step(body, [], [*rows.arrays, codes], [bf16(slots, total, rows.arrays[0].shape[2])])


def through(arrays):
    tiles, _, depth = arrays[0].shape

    def body(_, refs, outs, __):
        outs[0][...] = jnp.concatenate([ref[...] for ref in refs], axis=1) if len(refs) > 1 else refs[0][...]

    return Step(body, [], arrays, [bf16(tiles, sum(value.shape[1] for value in arrays), depth)])


def hold(value):
    def body(_, refs, outs, scratch):
        copy = pltpu.make_async_copy(refs[0], outs[0], scratch[0])
        copy.start()
        copy.wait()

    return Step(body, [], [], [bf16(*value.shape)], [pltpu.SemaphoreType.DMA(())], [value])


def products(codes, sources, blocks, ny, rows):
    nx, nc = len(sources), len(blocks)
    slots, depth, width = blocks[0].shape
    counts = [len(source.arrays) for source in sources]
    starts = [sum(counts[:d]) for d in range(nx + 1)]

    def body(_, refs, outs, __):
        block_refs = refs[starts[-1] : -1]
        x, c = lax.axis_index("blk") % nx, lax.axis_index("pair") % nc
        for k, tile in enumerate(read_codes(refs[-1], slots)):
            parts = [gather_rows(refs[starts[d] : starts[d + 1]], k if sources[d].packed else tile) for d in range(nx)]
            parts = [pick(x ^ i, parts) for i in range(nx)]
            columns = []
            for part in range(nc):
                pieces = [p[(s * nc + part) * rows : (s * nc + part + 1) * rows] for p in parts for s in range(ny)]
                columns.append(jnp.concatenate(pieces, axis=0))
            total = None
            for d in range(nc):
                term = jnp.dot(pick(c ^ d, columns), block_refs[d][k], preferred_element_type=jnp.float32)
                total = term if total is None else total + term
            for s in range(ny):
                pieces = [total[(i * ny + s) * rows : (i * ny + s + 1) * rows] for i in range(nx)]
                outs[s][k] = jnp.concatenate(pieces, axis=0).astype(outs[s].dtype)

    arrays = [value for source in sources for value in source.arrays] + [*blocks, codes]
    return Step(body, [], arrays, [bf16(slots, nx * rows, width)] * ny)


def route(tiles, keep, slot_tile, parts, tile_count, nx, nz):
    slots, rows, width = parts[0].shape
    owned = slot_tile.shape[0] // (nx * nz)
    per_tile = width // LANES

    def body(scalars, refs, outs, scratch):
        tiles_ref, keep_ref, slot_ref = scalars
        total = scratch[0]
        z, x = lax.axis_index("blk") // nx, lax.axis_index("blk") % nx
        total[...] = jnp.zeros_like(total)

        def add(k, _):
            value = refs[0][k].astype(jnp.float32)
            for ref in refs[1:]:
                value += ref[k].astype(jnp.float32)
            total[tiles_ref[1, k]] += value * keep_ref[k].astype(jnp.float32)
            return 0

        lax.fori_loop(0, slots, add, 0)
        for d in range(nx):
            for dz in range(nz):
                owner = (z ^ dz) * nx + (x ^ d)
                for i in range(owned):
                    tile = slot_ref[owner * owned + i]
                    a = lax.div(tile, per_tile)
                    column = pl.multiple_of(lax.rem(tile, per_tile) * LANES, LANES)
                    outs[d][dz * owned + i] = total[a, :, pl.ds(column, LANES)].astype(outs[d].dtype)

    scratch = [pltpu.VMEM((tile_count, rows, width), jnp.float32)]
    return Step(body, [tiles, keep, slot_tile], parts, [bf16(nz * owned, rows, LANES)] * nx, scratch)


def add_split(chunks, nz):
    tiles, rows, lanes = chunks[0][0].shape
    count, each = tiles // nz, len(chunks[0])

    def body(_, refs, outs, __):
        for i in range(len(chunks)):
            for e, out in enumerate(outs):
                span = slice(e * count, (e + 1) * count)
                value = refs[i * each][span].astype(jnp.float32)
                for part in refs[i * each + 1 : (i + 1) * each]:
                    value += part[span].astype(jnp.float32)
                out[:, i] = value.astype(out.dtype)

    flat = [part for chunk in chunks for part in chunk]
    return Step(body, [], flat, [bf16(count, len(chunks), rows, lanes)] * nz)


def fold(chunks, nz):
    tiles, rows, lanes = chunks[0][0].shape
    count, each = tiles // nz, len(chunks[0])

    def body(_, refs, outs, __):
        for i in range(len(chunks)):
            for e in range(nz):
                span = slice(e * count, (e + 1) * count)
                value = refs[i * each][span].astype(jnp.float32)
                for part in refs[i * each + 1 : (i + 1) * each]:
                    value += part[span].astype(jnp.float32)
                at = slice(e // 2 * count, (e // 2 + 1) * count)
                outs[e % 2][at, i ^ e % 2] = value.astype(outs[e % 2].dtype)

    flat = [part for chunk in chunks for part in chunk]
    return Step(body, [], flat, [bf16(nz // 2 * count, len(chunks), rows, lanes)] * 2)


def final_sum(received, nz, nx):
    owned, _, rows, lanes = received[0][0].shape

    def body(scalars, refs, outs, _):
        z = lax.axis_index("blk") // nx
        for ahead in range(nz):
            value = None
            for ref, (_, columns) in zip(refs, received, strict=True):
                if ahead in columns:
                    term = ref[:, columns.index(ahead)].astype(jnp.float32)
                    value = term if value is None else value + term
            outs[0][:, z ^ ahead] = value.astype(outs[0].dtype)

    return Step(body, [], [value for value, _ in received], [bf16(owned, nz, rows, lanes)])


def per_device(nz, nx, ny, nc, amplitudes, tile_mask, integrals, block_tiles, block_keep, slot_tile):
    pair = lax.axis_index("pair")
    y = pair // nc
    _, rows, tile_count, contracted = amplitudes.shape
    slots = block_keep.shape[0]
    columns = contracted // ny

    siblings = [pair_swap(integrals, 0, d, ny, nc) for d in range(1, nc)]
    blocks = [integrals]
    tiles = block_tiles.T

    masked = jnp.where(tile_mask[0][:, :, None] != 0, amplitudes[0], jnp.zeros((), amplitudes.dtype))
    masked = masked.transpose(1, 0, 2)
    depth = columns // nc
    pieces = []
    for d in range(ny):
        begin = (y ^ d) * columns
        pieces.append(
            jnp.concatenate([lax.dynamic_slice_in_dim(masked, begin + i * depth, depth, axis=2) for i in range(nc)], axis=1)
        )

    here, others, partial, by_owner, folded, received = {}, {}, {}, {}, {}, []
    last = []

    def run(name, due, *steps):
        nonlocal last
        results = launch(name, [step for step, _ in steps], last, due)
        last = list(results[0][:1])
        for (_, use), result in zip(steps, results, strict=True):
            use(result)

    def low_bits():
        return [d for d in range(1, nz) if d & -d == d]

    def do_first(s):
        def use(out):
            for d in range(1, nx):
                others[0][d - 1].append(blk_swap(out[0], 0, d, nz, nx))

        return through([from_y[s]]), use

    def do_along():
        def use(out):
            for d in reversed(low_bits()):
                here[d] = [blk_swap(out[0], d, 0, nz, nx)]

        return through(from_y), use

    def do_hold(i):
        return hold(siblings[i]), lambda out: blocks.append(out[0])

    def do_pack(d, i):
        def use(out):
            if i:
                others[d][i] = blk_swap(out[0], 0, i, nz, nx)
            else:
                own[d] = out[0]

        others.setdefault(d, {})
        if i:
            return pack(their_codes[i - 1], Rows(here[d], False), slots), use
        return pack(first, Rows(here[d], False), slots), use

    def do_forward(d):
        def use(out):
            for step in range(1, d & -d):
                if step & -step == step:
                    here[d | step] = [blk_swap(out[0], step, 0, nz, nx)]

        return through(here[d]), use

    def do_products(d):
        def use(out):
            partial[d] = [out[0]] + [pair_swap(out[i], i, 0, ny, nc) for i in range(1, ny)]

        if d:
            sources = [Rows([own[d]], True) if d in own else Rows(here[d], False)]
            sources += [Rows([others[d][i]], True) for i in range(1, nx)]
        else:
            sources = [Rows(from_y, False)] + [Rows(other, False) for other in others[0]]
        return products(first, sources, blocks, ny, rows), use

    def do_route(d):
        def use(out):
            by_owner[d] = [out[0]] + [blk_swap(out[i], 0, i, nz, nx) for i in range(1, nx)]

        return route(tiles, block_keep, slot_tile, partial[d], tile_count, nx, nz), use

    def do_add(group):
        def use(out):
            for e in reversed(range(nz)):
                received.append((blk_swap(out[e], e, 0, nz, nx) if e else out[0], [e ^ d for d in group]))

        return add_split([by_owner[d] for d in group], nz), use

    def do_fold(group):
        def use(out):
            folded[group] = [out[0], blk_swap(out[1], 1, 0, nz, nx)]

        return fold([by_owner[d] for d in group], nz), use

    def do_pass(group):
        def use(out):
            for e in range(0, nz, 2):
                received.append((blk_swap(out[e // 2], e, 0, nz, nx) if e else out[0], [e ^ d for d in group]))

        chunks = [[value.reshape(value.shape[0], -1, LANES) for value in folded[group]]]
        step = add_split(chunks, nz // 2)
        return step, lambda out: use([value.reshape(value.shape[0], len(group), -1, LANES) for value in out])

    from_y = [pieces[0]] + [pair_swap(pieces[d], d, 0, ny, nc) for d in range(1, ny)]
    codes = jnp.pad(tiles[:1].astype(jnp.bfloat16), ((0, nc * rows - 1), (0, depth - slots)))
    first = jnp.concatenate([pieces[0], codes[None]], axis=0)
    others[0] = [[blk_swap(first, 0, dx, nz, nx)] for dx in range(1, nx)]
    their_codes = [other[0] for other in others[0]]
    own = {}
    if nc > 1:
        run("hold", 8, *[do_hold(i) for i in range(nc - 1)])
    run("first", 20, *[do_first(s) for s in range(1, ny)], do_along())
    for due, slot in plan(nz):
        steps = []
        last = last + [value for what, g in slot if what == "sent" for value, _ in received[g * nz : (g + 1) * nz]]
        last = last + [value for what, d in slot if what == "came" for value in here[d]]
        last = last + [value for what, d in slot if what == "got" for value in partial[d][1:]]
        for what, d in slot:
            if what == "arrive":
                steps += [do_pack(d, i) for i in range(1, nx)] + ([do_pack(d, 0)] if len(here[d]) > 1 else [])
            elif what == "forward":
                steps.append(do_forward(d))
            elif what not in ("sent", "came", "got"):
                steps.append({"multiply": do_products, "route": do_route, "add": do_add, "fold": do_fold, "pass": do_pass}[what](d))
        run("_".join(what for what, _ in slot), due, *steps)
    out = launch("final_sum", [final_sum(received, nz, nx)], last, 2)[0][0]
    return out.reshape(out.shape[0], 1, out.shape[1] * out.shape[2], LANES)


def plan(nz):
    m, r, a, f, s = "multiply", "route", "arrive", "forward", "add"
    if nz == 4:
        return [
            (2, [(m, 0)]),
            (4, [(a, 1)]),
            (6, [(f, 2)]),
            (20, [(r, 0)]),
            (20, [(a, 2)]),
            (20, [(m, 1)]),
            (20, [(m, 2), (a, 3)]),
            (20, [(s, (0,))]),
            (20, [(r, 1)]),
            (20, [(m, 3)]),
            (20, [(r, 2), ("sent", 0)]),
            (20, [(s, (1,))]),
            (20, [(r, 3)]),
            (20, [(s, (2,))]),
            (20, [(s, (3,)), ("sent", 1)]),
        ]
    slots = [[(m, 0)]]
    for d in range(1, nz):
        slots.append([(a, d)] + ([(f, d)] if d & -d > 1 else []))
        slots.append([(m, d), (r, d - 1)])
    slots += [[(r, nz - 1)]] + [[(s, (d,))] for d in range(nz)]
    return [(5.0, slot) for slot in slots]


def solution(mesh):
    holders, pairs = mesh.shape["blk"], mesh.shape["pair"]
    nx = 1
    while (2 * nx) ** 2 <= holders:
        nx *= 2
    nc = 2 if pairs % 2 == 0 else 1
    placed = (
        P("pair", "blk", None, None),
        P("pair", "blk", None),
        P("blk", "pair", None),
        P("blk", None),
        P("blk"),
        P(),
    )
    return jax.shard_map(
        functools.partial(per_device, holders // nx, nx, pairs // nc, nc),
        mesh=mesh,
        in_specs=placed,
        out_specs=P("blk", "pair", None, None),
        check_vma=False,
    )
```
